256 devices in a mesh: dp: 32 (over z, x), tensor: 4 (over y_lo, core), tower: 2 (over y_hi).
Axes of the slice: x: 4, y: 4 (y_hi: 2, y_lo: 2; y = y_hi * 2 + y_lo), z: 8, core: 2. Of those that a mesh axis runs over, the one named last changes fastest.
Arguments:
- pooled: bfloat16 [8192, 1408], P(('dp', 'tower')), may hold values from -0.6 to 0.6
- w_up: bfloat16 [1408, 6144], P(None, 'tensor'), may hold values from -0.15625 to 0.15625
- w_down: bfloat16 [6144, 1408], P('tensor'), may hold values from -0.01953125 to 0.01953125
- text_embed: bfloat16 [8192, 1408], P(('dp', 'tensor', 'tower')), may hold values from -0.6 to 0.6
- scale_bias: float32 [2], replicated, may hold values from -4 to 2.2, as said below
Outputs:
- gradient_pooled_output: float32 [8192, 1408], P(('dp', 'tower'))
- grad_text: float32 [8192, 1408], P(('dp', 'tensor', 'tower'))
The draws below stay inside these ranges and needn't reach their ends.
Inputs may be any that keep to these rules, and one draw needn't show every extreme that they name: `scale_bias`: the first entry lies in 1.5 to 2.2 and the second in -4.0 to -2.0.
All inputs are finite; a program needn't handle non-finite values.
Results may differ from the reference program's by a relative error of at most 0.0055.
Values may be sent and summed in bfloat16 or wider, within the bound.
No kernel may reach another device: no remote copies, remote signals or barrier semaphores. Data moves between devices by JAX's collectives and lax.ppermute only.
A program may use at most 64 MiB of HBM per device.

```python
import math
import jax
import jax.numpy as jnp
from jax import lax

D = 1408
FF = 6144
BATCH = 8192


def concept_table(key):
    table_key = jax.random.fold_in(key, 101)
    return jnp.clip(jax.random.normal(table_key, (16, D), jnp.float32), -2.5, 2.5)


def concept_part(table, key, exponent):
    index_key, weight_key = jax.random.split(key, 2)
    concept_rows = jax.random.randint(index_key, (BATCH,), 0, 16)
    spread = jax.random.uniform(weight_key, (BATCH, 1), jnp.float32, -1.0, 1.0)
    spread = jnp.sign(spread) * jnp.abs(spread) ** exponent
    return 0.15 * spread * jnp.take(table, concept_rows, axis=0)


def draw_pooled(key, part):
    table = concept_table(key)
    key = jax.random.fold_in(key, 11)
    part_key, noise_key = jax.random.split(key, 2)
    shared = concept_part(table, part_key, 1.0)
    jitter = 0.05 * jnp.clip(jax.random.normal(noise_key, (BATCH, D), jnp.float32), -4.0, 4.0)
    return (shared + jitter).astype(jnp.bfloat16)


def draw_text_embed(key, part):
    table = concept_table(key)
    key = jax.random.fold_in(key, 13)
    part_key, noise_key = jax.random.split(key, 2)
    shared = concept_part(table, part_key, 1.0)
    jitter = 0.05 * jnp.clip(jax.random.normal(noise_key, (BATCH, D), jnp.float32), -4.0, 4.0)
    return (shared + jitter).astype(jnp.bfloat16)


def draw_scale_bias(key, part):
    key = jax.random.fold_in(key, 7)
    unit_draw = jax.random.uniform(key, (2,), jnp.float32)
    lower = jnp.array([1.5, -4.0], jnp.float32)
    upper = jnp.array([2.2, -2.0], jnp.float32)
    return lower + unit_draw * (upper - lower)


def levels(rng, shape, pieces, low, largest):
    def one(axis_at, blocks):
        heights = jax.random.uniform(jax.random.fold_in(jax.random.fold_in(rng, 6), axis_at), (blocks,), jnp.float32, low / len(pieces), largest / len(pieces))
        return jnp.repeat(jnp.exp(heights), shape[axis_at] // blocks).reshape((-1,) + (1,) * (len(shape) - axis_at - 1))

    loudness = one(*pieces[0])
    for cut in pieces[1:]:
        loudness = loudness * one(*cut)
    return loudness


def bell_draw(rng, extent, scale, limit, cuts=(), held_as=jnp.bfloat16):
    factor_of = levels(rng, extent, cuts, -0.22, 0.18) if cuts else 1.0
    values = jax.random.normal(rng, extent, jnp.float32) * scale * factor_of
    return jnp.minimum(jnp.maximum(values, -limit), limit).astype(held_as)


def setup_inputs(seed: int = 0) -> dict:
    key_list = jax.random.split(jax.random.key(seed), 6)
    pooled = draw_pooled(jax.random.fold_in(key_list[5], 71), 0)
    w_up = bell_draw(key_list[1], (D, FF), D ** -0.5, 0.15625, ((1, 4),))
    w_down = bell_draw(key_list[2], (FF, D), (16 * FF) ** -0.5, 0.01953125, ((0, 4),))
    text_embed = draw_text_embed(jax.random.fold_in(key_list[5], 71), 0)
    scale_bias = draw_scale_bias(jax.random.fold_in(key_list[5], 71), 0)
    return dict(pooled=pooled, w_up=w_up, w_down=w_down, text_embed=text_embed, scale_bias=scale_bias)


def reference(pooled, w_up, w_down, text_embed, scale_bias):
    activation = pooled.astype(jnp.float32)
    row_mean = lax.optimization_barrier(jnp.mean(activation, axis=1, keepdims=True))
    mean_removed = activation - row_mean
    variance = lax.optimization_barrier(jnp.mean(mean_removed * mean_removed, axis=1, keepdims=True))
    inverse_deviation = lax.rsqrt(variance + 1e-06)
    standardized_input = mean_removed * inverse_deviation
    layernorm_output = standardized_input.astype(jnp.bfloat16)
    pre_act = jnp.dot(layernorm_output, w_up, preferred_element_type=jnp.float32)
    hidden = jax.nn.gelu(pre_act).astype(jnp.bfloat16)
    resid = activation + jnp.dot(hidden, w_down, preferred_element_type=jnp.float32)
    inv_img = lax.rsqrt(lax.optimization_barrier(jnp.sum(resid * resid, axis=1, keepdims=True)) + 1e-06)
    image_emb = resid * inv_img
    image_half = image_emb.astype(jnp.bfloat16)
    text_full = text_embed.astype(jnp.float32)
    inv_txt = lax.rsqrt(lax.optimization_barrier(jnp.sum(text_full * text_full, axis=1, keepdims=True)) + 1e-06)
    text_unit = text_full * inv_txt
    text_half = text_unit.astype(jnp.bfloat16)
    logit_scale = jnp.exp(scale_bias[0])
    logit_bias = scale_bias[1]
    block_rows = math.gcd(BATCH, 512)
    block_count = BATCH // block_rows
    image_blocks = image_half.reshape(block_count, block_rows, D)
    text_ids = jnp.arange(BATCH, dtype=jnp.int32)

    def one_block(carry, item):
        block_index, block_images = item
        scores = lax.dot_general(block_images, text_half, (((1,), (1,)), ((), ())), preferred_element_type=jnp.float32)
        logits = logit_scale * scores + logit_bias
        image_ids = block_index * block_rows + jnp.arange(block_rows, dtype=jnp.int32)
        pair_sign = jnp.where(image_ids[:, None] == text_ids[None, :], 1.0, -1.0).astype(jnp.float32)
        pair_grad = -pair_sign * jax.nn.sigmoid(-pair_sign * logits)
        coef_half = (pair_grad * logit_scale).astype(jnp.bfloat16)
        block_grad = jnp.dot(coef_half, text_half, preferred_element_type=jnp.float32)
        carry = carry + lax.dot_general(coef_half, block_images, (((0,), (0,)), ((), ())), preferred_element_type=jnp.float32)
        return (carry, block_grad)
    grad_unit, grad_blocks = lax.scan(one_block, jnp.zeros((BATCH, D), jnp.float32), (jnp.arange(block_count, dtype=jnp.int32), image_blocks))
    grad_emb = grad_blocks.reshape(BATCH, D)
    grad_text = (grad_unit - text_unit * lax.optimization_barrier(jnp.sum(text_unit * grad_unit, axis=1, keepdims=True))) * inv_txt
    gradient_residual = (grad_emb - image_emb * lax.optimization_barrier(jnp.sum(image_emb * grad_emb, axis=1, keepdims=True))) * inv_img
    resid_half = gradient_residual.astype(jnp.bfloat16)
    grad_hidden = lax.dot_general(resid_half, w_down, (((1,), (1,)), ((), ())), preferred_element_type=jnp.float32)
    _, gelu_back = jax.vjp(jax.nn.gelu, pre_act)
    grad_pre = gelu_back(grad_hidden)[0].astype(jnp.bfloat16)
    gradient_layernormed = lax.dot_general(grad_pre, w_up, (((1,), (1,)), ((), ())), preferred_element_type=jnp.float32)
    layernorm_output_mean = lax.optimization_barrier(jnp.mean(gradient_layernormed, axis=1, keepdims=True))
    layernorm_projection = lax.optimization_barrier(jnp.mean(gradient_layernormed * standardized_input, axis=1, keepdims=True))
    gradient_pooled_output = gradient_residual + inverse_deviation * (gradient_layernormed - layernorm_output_mean - standardized_input * layernorm_projection)
    return (gradient_pooled_output, grad_text)
```

```python
import jax
import jax.numpy as jnp
from jax import lax
from jax.sharding import Mesh, PartitionSpec as P

F32 = jnp.float32
BF16 = jnp.bfloat16


def swap(value, axis):
    return lax.ppermute(value, axis, [(0, 1), (1, 0)])


def shift(value, axis, by):
    count = lax.axis_size(axis)
    return lax.ppermute(value, axis, [(i, (i + by) % count) for i in range(count)])


def matmul(a, b, dims):
    return lax.dot_general(a, b, (dims, ((), ())), preferred_element_type=F32)


def local(pooled, w_up, w_down, text_embed, scale_bias):
    z, x, yl, c, yh = (lax.axis_index(a) for a in ("z", "x", "yl", "c", "yh"))
    text_full = text_embed.astype(F32)
    inv_txt = lax.rsqrt(jnp.sum(text_full * text_full, axis=1, keepdims=True) + 1e-06)
    text_unit = text_full * inv_txt
    text_half = text_unit.astype(BF16)
    texts_own = lax.all_gather(text_half, "z", axis=0, tiled=True)
    texts = jnp.concatenate([texts_own, swap(texts_own, "yh")], axis=0)

    half = pooled.shape[0] // 2
    mine = lax.dynamic_slice_in_dim(pooled, c * half, half, 0)
    others = lax.dynamic_slice_in_dim(pooled, (1 - c) * half, half, 0)
    activation = jnp.concatenate([mine, others], axis=0).astype(F32)
    row_mean = jnp.mean(activation, axis=1, keepdims=True)
    mean_removed = activation - row_mean
    variance = jnp.mean(mean_removed * mean_removed, axis=1, keepdims=True)
    inverse_deviation = lax.rsqrt(variance + 1e-06)
    standardized = mean_removed * inverse_deviation
    normed = standardized.astype(BF16)
    pre_act = matmul(normed, w_up, ((1,), (0,)))
    hidden = jax.nn.gelu(pre_act).astype(BF16)
    partial = matmul(hidden, w_down, ((1,), (0,)))
    branch = (partial[:half] + swap(partial[half:], "c")).astype(BF16)
    branch = branch.astype(F32) + swap(branch, "yl").astype(F32)
    resid = activation[:half] + branch
    inv_img = lax.rsqrt(jnp.sum(resid * resid, axis=1, keepdims=True) + 1e-06)
    image_emb = resid * inv_img
    image_half = image_emb.astype(BF16)
    by_shift = {k: shift(image_half, "x", k) for k in (2, 1, 3)}
    images_own = jnp.concatenate([image_half, by_shift[1], by_shift[2], by_shift[3]], axis=0)
    images = jnp.concatenate([images_own, swap(images_own, "c")], axis=0)

    row = jnp.arange(images.shape[0], dtype=jnp.int32)
    from_x = (x - (row // half) % 4 + 4) % 4
    from_c = jnp.where(row < 4 * half, c, 1 - c)
    image_ids = ((z * 4 + from_x) * 2 + yh) * (2 * half) + from_c * half + row % half
    few = text_half.shape[0]
    col = jnp.arange(texts.shape[0], dtype=jnp.int32)
    from_z = (col // few) % 8
    from_yh = jnp.where(col < 8 * few, yh, 1 - yh)
    text_ids = ((((from_z * 4 + x) * 2 + yl) * 2 + c) * 2 + from_yh) * few + col % few
    logit_scale = jnp.exp(scale_bias[0])
    logits = logit_scale * matmul(images, texts, ((1,), (1,))) + scale_bias[1]
    pair_sign = jnp.where(image_ids[:, None] == text_ids[None, :], 1.0, -1.0).astype(F32)
    pair_grad = -pair_sign * jax.nn.sigmoid(-pair_sign * logits)
    coef = (pair_grad * logit_scale).astype(BF16)
    grad_emb = matmul(coef, texts, ((1,), (0,)))
    grad_unit = matmul(coef, images, ((0,), (0,)))

    quad = 4 * half
    grad_emb = grad_emb[:quad] + swap(grad_emb[quad:], "c")
    sent = grad_emb.astype(BF16)
    total = grad_emb[:half]
    for k in (2, 1, 3):
        total = total + shift(sent[k * half : (k + 1) * half], "x", -k).astype(F32)
    total = total.astype(BF16)
    total = total.astype(F32) + swap(total, "yl").astype(F32)
    grad_resid = (total - image_emb * jnp.sum(image_emb * total, axis=1, keepdims=True)) * inv_img
    resid_half = grad_resid.astype(BF16)
    resid_half = jnp.concatenate([resid_half, swap(resid_half, "c")], axis=0)
    grad_hidden = matmul(resid_half, w_down, ((1,), (1,)))
    _, gelu_back = jax.vjp(jax.nn.gelu, pre_act)
    grad_pre = gelu_back(grad_hidden)[0].astype(BF16)
    partial_normed = matmul(grad_pre, w_up, ((1,), (1,)))
    normed_sum = (partial_normed[:half] + swap(partial_normed[half:], "c")).astype(BF16)
    normed_sum = normed_sum.astype(F32) + swap(normed_sum, "yl").astype(F32)
    mean_one = jnp.mean(normed_sum, axis=1, keepdims=True)
    xhat = standardized[:half]
    mean_two = jnp.mean(normed_sum * xhat, axis=1, keepdims=True)
    mine_out = grad_resid + inverse_deviation[:half] * (normed_sum - mean_one - xhat * mean_two)
    other_out = swap(mine_out, "c")
    first = jnp.where(c == 0, mine_out, other_out)
    second = jnp.where(c == 0, other_out, mine_out)
    gradient_pooled_output = jnp.concatenate([first, second], axis=0)

    oct_ = 8 * few
    unit_sum = grad_unit[:oct_] + swap(grad_unit[oct_:].astype(BF16), "yh").astype(F32)
    unit_sent = unit_sum.astype(BF16)
    grad_own = lax.dynamic_slice_in_dim(unit_sum, z * few, few, 0)
    for k in (4, 3, 5, 2, 6, 1, 7):
        piece = lax.dynamic_slice_in_dim(unit_sent, (z + k) % 8 * few, few, 0)
        grad_own = grad_own + shift(piece, "z", k).astype(F32)
    grad_text = (grad_own - text_unit * jnp.sum(text_unit * grad_own, axis=1, keepdims=True)) * inv_txt
    return (gradient_pooled_output, grad_text)


def solution(mesh):
    fine = Mesh(mesh.devices.reshape(8, 4, 2, 2, 2), ("z", "x", "yl", "c", "yh"))
    images = P(("z", "x", "yh"), None)
    texts = P(("z", "x", "yl", "c", "yh"), None)
    return jax.shard_map(
        local,
        mesh=fine,
        in_specs=(images, P(None, ("yl", "c")), P(("yl", "c"), None), texts, P()),
        out_specs=(images, texts),
        check_vma=False,
    )
```

```python
import jax
import jax.numpy as jnp
from jax import lax
from jax.sharding import Mesh, PartitionSpec as P

F32 = jnp.float32
BF16 = jnp.bfloat16


def swap(value, axis):
    return lax.ppermute(value, axis, [(0, 1), (1, 0)])


def shift(value, axis, by):
    count = lax.axis_size(axis)
    return lax.ppermute(value, axis, [(i, (i + by) % count) for i in range(count)])


def across(value):
    return lax.ppermute(
        value, ("z", "yh"), [(2 * i + j, 2 * ((i + 4) % 8) + 1 - j) for i in range(8) for j in range(2)]
    )


def sides(value, by):
    hops = [((i, j), ((i + (by if j == 0 else -by)) % 4, j)) for i in range(4) for j in range(2)]
    return lax.ppermute(value, ("x", "c"), [(2 * a + b, 2 * p + q) for (a, b), (p, q) in hops])


def apart(value, by):
    hops = [((i, j), ((i + (by if j == 0 else -by)) % 8, j)) for i in range(8) for j in range(2)]
    return lax.ppermute(value, ("z", "c"), [(2 * a + b, 2 * p + q) for (a, b), (p, q) in hops])


QUAD = [(0, 0), (4, 0), (0, 1), (4, 1)]
TEXT_BLOCKS = (
    QUAD
    + [(dz + 1, flip) for dz, flip in QUAD]
    + [(dz - 1, flip) for dz, flip in QUAD]
)


def after(values, first):
    return lax.optimization_barrier((values, first))[0]


def matmul(a, b, dims):
    return lax.dot_general(a, b, (dims, ((), ())), preferred_element_type=F32)


def local(pooled, w_up, w_down, text_embed, scale_bias):
    z, x, yl, c, yh = (lax.axis_index(a) for a in ("z", "x", "yl", "c", "yh"))
    text_full = text_embed.astype(F32)
    inv_txt = lax.rsqrt(jnp.sum(text_full * text_full, axis=1, keepdims=True) + 1e-06)
    text_unit = text_full * inv_txt
    text_half = text_unit.astype(BF16)
    near = [shift(text_half, "z", 4), swap(text_half, "yh"), across(text_half)]

    half = pooled.shape[0] // 2
    mine = lax.dynamic_slice_in_dim(pooled, c * half, half, 0)
    others = lax.dynamic_slice_in_dim(pooled, (1 - c) * half, half, 0)
    activation = jnp.concatenate([mine, others], axis=0).astype(F32)
    row_mean = jnp.mean(activation, axis=1, keepdims=True)
    mean_removed = activation - row_mean
    variance = jnp.mean(mean_removed * mean_removed, axis=1, keepdims=True)
    inverse_deviation = lax.rsqrt(variance + 1e-06)
    standardized = mean_removed * inverse_deviation
    normed = standardized.astype(BF16)
    pre_act = matmul(normed, w_up, ((1,), (0,)))
    hidden = jax.nn.gelu(pre_act).astype(BF16)
    partial = matmul(hidden, w_down, ((1,), (0,)))
    branch = (partial[:half] + swap(partial[half:], "c")).astype(BF16)
    near = after(near, branch)
    four = jnp.concatenate([text_half] + near, axis=0)
    texts_in = [shift(four, "z", 1), shift(four, "z", -1), apart(four, 2)]
    branch = branch.astype(F32) + swap(branch, "yl").astype(F32)
    resid = activation[:half] + branch
    inv_img = lax.rsqrt(jnp.sum(resid * resid, axis=1, keepdims=True) + 1e-06)
    image_emb = resid * inv_img
    image_half = image_emb.astype(BF16)
    rows_own = lax.all_gather(image_half, "x", axis=0, tiled=True)
    rows_other = swap(rows_own, "c")
    side = 1 - 2 * c
    image_blocks = [(0, 0), (side, 0), (side, 1), (2, 0), (-side, 1), (-side, 0), (2, 1), (0, 1)]
    images = jnp.concatenate(
        [
            lax.dynamic_slice_in_dim(rows_other if other else rows_own, (x - dx + 4) % 4 * half, half, 0)
            for dx, other in image_blocks
        ],
        axis=0,
    )
    texts_in = after(texts_in, rows_own)
    texts = jnp.concatenate([four] + texts_in, axis=0)

    image_ids = jnp.concatenate(
        [
            ((z * 4 + (x - dx + 4) % 4) * 2 + yh) * (2 * half) + (c ^ other) * half + jnp.arange(half, dtype=jnp.int32)
            for dx, other in image_blocks
        ]
    )
    few = text_half.shape[0]
    col = jnp.arange(texts.shape[0], dtype=jnp.int32)
    back = jnp.asarray([dz for dz, _ in TEXT_BLOCKS + QUAD], jnp.int32)
    back = back + jnp.where(jnp.arange(16) >= 12, 2 - 4 * c, 0)
    flip = jnp.asarray([f for _, f in TEXT_BLOCKS + QUAD], jnp.int32)
    from_z = (z - jnp.repeat(back, few) + 8) % 8
    from_yh = yh ^ jnp.repeat(flip, few)
    text_ids = ((((from_z * 4 + x) * 2 + yl) * 2 + c) * 2 + from_yh) * few + col % few
    logit_scale = jnp.exp(scale_bias[0])
    logits = logit_scale * matmul(images, texts, ((1,), (1,))) + scale_bias[1]
    pair_sign = jnp.where(image_ids[:, None] == text_ids[None, :], 1.0, -1.0).astype(F32)
    pair_grad = -pair_sign * jax.nn.sigmoid(-pair_sign * logits)
    coef = (pair_grad * logit_scale).astype(BF16)
    grad_emb = matmul(coef, texts, ((1,), (0,)))
    grad_unit = matmul(coef, images, ((0,), (0,)))

    unit_sent = grad_unit.astype(BF16)
    four = 4 * few
    unit_in = [
        shift(unit_sent[four : 2 * four], "z", -1),
        shift(unit_sent[2 * four : 3 * four], "z", 1),
        apart(unit_sent[3 * four :], -2),
    ]

    quad = 4 * half
    own_emb = grad_emb[:quad]
    other_emb = jnp.concatenate([grad_emb[2 * quad - half :], grad_emb[quad : 2 * quad - half]], axis=0)
    other_emb = after(other_emb, unit_sent)
    grad_emb = own_emb + swap(other_emb, "c")
    sent = grad_emb.astype(BF16)
    near = sides(sent[half : 3 * half], -1)
    total = grad_emb[:half] + shift(sent[3 * half :], "x", -2).astype(F32)
    near, unit_in = lax.optimization_barrier((near, unit_in))
    total = total + near[:half].astype(F32) + swap(near[half:], "c").astype(F32)
    total = total.astype(BF16)
    below, above, far = (value.astype(F32) for value in unit_in)
    unit_sum = grad_unit[:four] + below + above + far
    unit_flipped = swap(unit_sum[2 * few :].astype(BF16), "yh")
    total = total.astype(F32) + swap(total, "yl").astype(F32)
    grad_resid = (total - image_emb * jnp.sum(image_emb * total, axis=1, keepdims=True)) * inv_img
    resid_half = grad_resid.astype(BF16)
    resid_half = jnp.concatenate([resid_half, swap(resid_half, "c")], axis=0)
    grad_hidden = matmul(resid_half, w_down, ((1,), (1,)))
    _, gelu_back = jax.vjp(jax.nn.gelu, pre_act)
    grad_pre = gelu_back(grad_hidden)[0].astype(BF16)
    partial_normed = matmul(grad_pre, w_up, ((1,), (1,)))
    unit_flipped = after(unit_flipped, partial_normed)
    unit_sum = unit_sum[: 2 * few] + unit_flipped.astype(F32)
    unit_far = shift(unit_sum[few:].astype(BF16), "z", 4)
    normed_sum = (partial_normed[:half] + swap(partial_normed[half:], "c")).astype(BF16)
    normed_sum = normed_sum.astype(F32) + swap(normed_sum, "yl").astype(F32)
    mean_one = jnp.mean(normed_sum, axis=1, keepdims=True)
    xhat = standardized[:half]
    mean_two = jnp.mean(normed_sum * xhat, axis=1, keepdims=True)
    mine_out = grad_resid + inverse_deviation[:half] * (normed_sum - mean_one - xhat * mean_two)
    other_out = swap(mine_out, "c")
    first = jnp.where(c == 0, mine_out, other_out)
    second = jnp.where(c == 0, other_out, mine_out)
    gradient_pooled_output = jnp.concatenate([first, second], axis=0)

    grad_own = unit_sum[:few] + after(unit_far, mine_out).astype(F32)
    grad_text = (grad_own - text_unit * jnp.sum(text_unit * grad_own, axis=1, keepdims=True)) * inv_txt
    return (gradient_pooled_output, grad_text)


def solution(mesh):
    fine = Mesh(mesh.devices.reshape(8, 4, 2, 2, 2), ("z", "x", "yl", "c", "yh"))
    images = P(("z", "x", "yh"), None)
    texts = P(("z", "x", "yl", "c", "yh"), None)
    return jax.shard_map(
        local,
        mesh=fine,
        in_specs=(images, P(None, ("yl", "c")), P(("yl", "c"), None), texts, P()),
        out_specs=(images, texts),
        check_vma=False,
    )
```

```python
import jax
import jax.numpy as jnp
from jax import lax
from jax.experimental import pallas as pl
from jax.experimental.pallas import tpu as pltpu
from jax.sharding import Mesh, PartitionSpec as P

F32 = jnp.float32
BF16 = jnp.bfloat16


def swap(value, axis):
    return lax.ppermute(value, axis, [(0, 1), (1, 0)])


def shift(value, axis, by):
    count = lax.axis_size(axis)
    return lax.ppermute(value, axis, [(i, (i + by) % count) for i in range(count)])


def across(value):
    return lax.ppermute(
        value, ("z", "yh"), [(2 * i + j, 2 * ((i + 4) % 8) + 1 - j) for i in range(8) for j in range(2)]
    )


def sides(value, by):
    hops = [((i, j), ((i + (by if j == 0 else -by)) % 4, j)) for i in range(4) for j in range(2)]
    return lax.ppermute(value, ("x", "c"), [(2 * a + b, 2 * p + q) for (a, b), (p, q) in hops])


def apart(value, by):
    hops = [((i, j), ((i + (by if j == 0 else -by)) % 8, j)) for i in range(8) for j in range(2)]
    return lax.ppermute(value, ("z", "c"), [(2 * a + b, 2 * p + q) for (a, b), (p, q) in hops])


QUAD = [(0, 0), (4, 0), (0, 1), (4, 1)]
TEXT_BLOCKS = (
    QUAD
    + [(dz + 1, flip) for dz, flip in QUAD]
    + [(dz - 1, flip) for dz, flip in QUAD]
)


def after(values, first):
    return lax.optimization_barrier((values, first))[0]


def matmul(a, b, dims):
    return lax.dot_general(a, b, (dims, ((), ())), preferred_element_type=F32)


STEP = 512
VMEM = pl.BlockSpec(memory_space=pltpu.VMEM)
SMEM = pl.BlockSpec(memory_space=pltpu.SMEM)
HBM = pl.BlockSpec(memory_space=pltpu.HBM)


def weight_copies(up_hbm, down_hbm, up, down, sems):
    steps = up.shape[0]
    ups = [
        pltpu.make_async_copy(up_hbm.at[:, pl.ds(k * STEP, STEP)], up.at[k], sems.at[k]) for k in range(steps)
    ]
    downs = [
        pltpu.make_async_copy(down_hbm.at[pl.ds(k * STEP, STEP)], down.at[k], sems.at[steps + k])
        for k in range(steps)
    ]
    return ups, downs


def split_rows(core, total, mine, others):
    half = mine.shape[0]
    mine[...] = total[pl.ds(pl.multiple_of(core * half, half), half), :]
    others[...] = total[pl.ds(pl.multiple_of((1 - core) * half, half), half), :]


def forward_kernel(core, pooled, text, up_hbm, down_hbm, mine, others, pre_act, text_half, inv_txt, up, down, total, sems):
    ups, downs = weight_copies(up_hbm, down_hbm, up, down, sems)
    for first, second in zip(ups, downs):
        first.start()
        second.start()
    full = text[...].astype(F32)
    inv = lax.rsqrt(jnp.sum(full * full, axis=1, keepdims=True) + 1e-06)
    text_half[...] = (full * inv).astype(BF16)
    inv_txt[...] = inv
    activation = pooled[...].astype(F32)
    mean_removed = activation - jnp.mean(activation, axis=1, keepdims=True)
    variance = jnp.mean(mean_removed * mean_removed, axis=1, keepdims=True)
    normed = (mean_removed * lax.rsqrt(variance + 1e-06)).astype(BF16)
    for k in range(len(ups)):
        ups[k].wait()
        pre = matmul(normed, up[k], ((1,), (0,)))
        pre_act[:, pl.ds(k * STEP, STEP)] = pre
        hidden = jax.nn.gelu(pre).astype(BF16)
        downs[k].wait()
        part = matmul(hidden, down[k], ((1,), (0,)))
        total[...] = part if k == 0 else total[...] + part
    split_rows(core[0], total, mine, others)


def backward_kernel(core, grad_mine, grad_others, pre_act, up_hbm, down_hbm, mine, others, up, down, grad, total, sems):
    ups, downs = weight_copies(up_hbm, down_hbm, up, down, sems)
    for first, second in zip(downs, ups):
        first.start()
        second.start()
    half = mine.shape[0]
    grad[pl.ds(pl.multiple_of(core[0] * half, half), half), :] = grad_mine[...]
    grad[pl.ds(pl.multiple_of((1 - core[0]) * half, half), half), :] = grad_others[...]
    for k in range(len(ups)):
        downs[k].wait()
        grad_hidden = matmul(grad[...], down[k], ((1,), (1,)))
        pre = pre_act[:, pl.ds(k * STEP, STEP)]
        root = 0.7978845608028654
        bend = jnp.tanh(root * (pre + 0.044715 * (pre * pre * pre)))
        slope = 0.5 * (1.0 + bend) + (0.5 * root) * pre * (1.0 - bend * bend) * (1.0 + 0.134145 * (pre * pre))
        grad_pre = (grad_hidden * slope).astype(BF16)
        ups[k].wait()
        part = matmul(grad_pre, up[k], ((1,), (1,)))
        total[...] = part if k == 0 else total[...] + part
    split_rows(core[0], total, mine, others)


def mlp_scratch(rows, width, hidden):
    steps = hidden // STEP
    return [
        pltpu.VMEM((steps, width, STEP), BF16),
        pltpu.VMEM((steps, STEP, width), BF16),
        pltpu.VMEM((rows, width), F32),
        pltpu.SemaphoreType.DMA((2 * steps,)),
    ]


def mlp_call(kernel, specs, shapes, scratch, flops, grant):
    return pl.pallas_call(
        kernel,
        in_specs=specs,
        out_specs=[VMEM] * len(shapes),
        out_shape=[jax.ShapeDtypeStruct(shape, dtype) for shape, dtype in shapes],
        scratch_shapes=scratch,
        compiler_params=pltpu.CompilerParams(vmem_limit_bytes=grant * 1024 * 1024),
        cost_estimate=pl.CostEstimate(flops=6 * flops, bytes_accessed=10_000_000, transcendentals=0),
    )


def local(pooled, w_up, w_down, text_embed, scale_bias):
    z, x, yl, c, yh = (lax.axis_index(a) for a in ("z", "x", "yl", "c", "yh"))

    rows, width = pooled.shape
    half = rows // 2
    ff = w_up.shape[1]
    core = c.astype(jnp.int32).reshape(1)
    partial_mine, partial_others, pre_act, text_half, inv_txt = mlp_call(
        forward_kernel,
        [SMEM, VMEM, VMEM, HBM, HBM],
        [
            ((half, width), F32),
            ((half, width), F32),
            ((rows, ff), F32),
            (text_embed.shape, BF16),
            ((text_embed.shape[0], 1), F32),
        ],
        mlp_scratch(rows, width, ff),
        4 * rows * width * ff,
        60,
    )(core, pooled, text_embed, w_up, w_down)
    near = [shift(text_half, "z", 4), swap(text_half, "yh"), across(text_half)]
    branch = (partial_mine + swap(partial_others, "c")).astype(BF16)
    activation = lax.dynamic_slice_in_dim(pooled, c * half, half, 0).astype(F32)
    row_mean = jnp.mean(activation, axis=1, keepdims=True)
    mean_removed = activation - row_mean
    variance = jnp.mean(mean_removed * mean_removed, axis=1, keepdims=True)
    inverse_deviation = lax.rsqrt(variance + 1e-06)
    xhat = mean_removed * inverse_deviation
    four = jnp.concatenate(after([text_half] + near, branch), axis=0)
    texts_in = [shift(four, "z", 1), shift(four, "z", -1), apart(four, 2)]
    branch = branch.astype(F32) + swap(branch, "yl").astype(F32)
    resid = activation + branch
    inv_img = lax.rsqrt(jnp.sum(resid * resid, axis=1, keepdims=True) + 1e-06)
    image_emb = resid * inv_img
    image_half = image_emb.astype(BF16)
    rows_own = lax.all_gather(image_half, "x", axis=0, tiled=True)
    rows_other = swap(rows_own, "c")
    side = 1 - 2 * c
    image_blocks = [(0, 0), (side, 0), (side, 1), (2, 0), (-side, 1), (-side, 0), (2, 1), (0, 1)]
    images = jnp.concatenate(
        [
            lax.dynamic_slice_in_dim(rows_other if other else rows_own, (x - dx + 4) % 4 * half, half, 0)
            for dx, other in image_blocks
        ],
        axis=0,
    )
    texts_in = after(texts_in, rows_own)
    texts = jnp.concatenate([four] + texts_in, axis=0)

    image_ids = jnp.concatenate(
        [
            ((z * 4 + (x - dx + 4) % 4) * 2 + yh) * (2 * half) + (c ^ other) * half + jnp.arange(half, dtype=jnp.int32)
            for dx, other in image_blocks
        ]
    )
    few = text_half.shape[0]
    col = jnp.arange(texts.shape[0], dtype=jnp.int32)
    back = jnp.asarray([dz for dz, _ in TEXT_BLOCKS + QUAD], jnp.int32)
    back = back + jnp.where(jnp.arange(16) >= 12, 2 - 4 * c, 0)
    flip = jnp.asarray([f for _, f in TEXT_BLOCKS + QUAD], jnp.int32)
    from_z = (z - jnp.repeat(back, few) + 8) % 8
    from_yh = yh ^ jnp.repeat(flip, few)
    text_ids = ((((from_z * 4 + x) * 2 + yl) * 2 + c) * 2 + from_yh) * few + col % few
    logit_scale = jnp.exp(scale_bias[0])
    logits = logit_scale * matmul(images, texts, ((1,), (1,))) + scale_bias[1]
    pair_sign = jnp.where(image_ids[:, None] == text_ids[None, :], 1.0, -1.0).astype(F32)
    pair_grad = -pair_sign * jax.nn.sigmoid(-pair_sign * logits)
    coef = (pair_grad * logit_scale).astype(BF16)
    quad = 4 * half
    other_emb = matmul(
        jnp.concatenate([coef[2 * quad - half :], coef[quad : 2 * quad - half]], axis=0), texts, ((1,), (0,))
    )
    swapped_emb = swap(other_emb, "c")
    own_emb = matmul(coef[:quad], texts, ((1,), (0,)))
    grad_unit = matmul(coef, images, ((0,), (0,)))

    unit_sent = grad_unit.astype(BF16)
    four = 4 * few
    unit_in = [
        shift(unit_sent[four : 2 * four], "z", -1),
        shift(unit_sent[2 * four : 3 * four], "z", 1),
        apart(unit_sent[3 * four :], -2),
    ]

    grad_emb = own_emb + after(swapped_emb, unit_sent)
    sent = grad_emb.astype(BF16)
    near = sides(sent[half : 3 * half], -1)
    total = grad_emb[:half] + shift(sent[3 * half :], "x", -2).astype(F32)
    near, unit_in = lax.optimization_barrier((near, unit_in))
    total = total + near[:half].astype(F32) + swap(near[half:], "c").astype(F32)
    total = total.astype(BF16)
    below, above, far = (value.astype(F32) for value in unit_in)
    unit_sum = grad_unit[:four] + below + above + far
    unit_sent = unit_sum[2 * few :].astype(BF16)
    unit_flipped = swap(unit_sent, "yh")
    total = total.astype(F32) + swap(total, "yl").astype(F32)
    grad_resid = (total - image_emb * jnp.sum(image_emb * total, axis=1, keepdims=True)) * inv_img
    resid_half = after(grad_resid.astype(BF16), unit_sent)
    scratch = mlp_scratch(rows, width, ff)
    normed_mine, normed_others = mlp_call(
        backward_kernel,
        [SMEM, VMEM, VMEM, VMEM, HBM, HBM],
        [((half, width), F32), ((half, width), F32)],
        scratch[:2] + [pltpu.VMEM((rows, width), BF16)] + scratch[2:],
        4 * rows * width * ff,
        20,
    )(core, resid_half, swap(resid_half, "c"), pre_act, w_up, w_down)
    normed_others, unit_flipped = lax.optimization_barrier((normed_others, unit_flipped))
    unit_sum = unit_sum[: 2 * few] + unit_flipped.astype(F32)
    unit_far = shift(unit_sum[few:].astype(BF16), "z", 4)
    normed_sum = (normed_mine + swap(normed_others, "c")).astype(BF16)
    normed_sum = normed_sum.astype(F32) + swap(normed_sum, "yl").astype(F32)
    mean_one = jnp.mean(normed_sum, axis=1, keepdims=True)
    mean_two = jnp.mean(normed_sum * xhat, axis=1, keepdims=True)
    mine_out = grad_resid + inverse_deviation * (normed_sum - mean_one - xhat * mean_two)
    other_out = swap(mine_out, "c")
    first = jnp.where(c == 0, mine_out, other_out)
    second = jnp.where(c == 0, other_out, mine_out)
    gradient_pooled_output = jnp.concatenate([first, second], axis=0)

    grad_own = unit_sum[:few] + after(unit_far, mine_out).astype(F32)
    text_unit = text_embed.astype(F32) * inv_txt
    grad_text = (grad_own - text_unit * jnp.sum(text_unit * grad_own, axis=1, keepdims=True)) * inv_txt
    return (gradient_pooled_output, grad_text)


def solution(mesh):
    fine = Mesh(mesh.devices.reshape(8, 4, 2, 2, 2), ("z", "x", "yl", "c", "yh"))
    images = P(("z", "x", "yh"), None)
    texts = P(("z", "x", "yl", "c", "yh"), None)
    return jax.shard_map(
        local,
        mesh=fine,
        in_specs=(images, P(None, ("yl", "c")), P(("yl", "c"), None), texts, P()),
        out_specs=(images, texts),
        check_vma=False,
    )
```

```python
import jax
import jax.numpy as jnp
from jax import lax
from jax.experimental import pallas as pl
from jax.experimental.pallas import tpu as pltpu
from jax.sharding import Mesh, PartitionSpec as P

F32 = jnp.float32
BF16 = jnp.bfloat16


def swap(value, axis):
    return lax.ppermute(value, axis, [(0, 1), (1, 0)])


def shift(value, axis, by):
    count = lax.axis_size(axis)
    return lax.ppermute(value, axis, [(i, (i + by) % count) for i in range(count)])


def across(value):
    return lax.ppermute(
        value, ("z", "yh"), [(2 * i + j, 2 * ((i + 4) % 8) + 1 - j) for i in range(8) for j in range(2)]
    )


def sides(value, by):
    hops = [((i, j), ((i + (by if j == 0 else -by)) % 4, j)) for i in range(4) for j in range(2)]
    return lax.ppermute(value, ("x", "c"), [(2 * a + b, 2 * p + q) for (a, b), (p, q) in hops])


def apart(value, by, flip=0):
    hops = []
    for i in range(8):
        for j in range(2):
            to = (i + (by if j == 0 else -by)) % 8
            hops += [((2 * i + j) * 2 + k, (2 * to + j) * 2 + (k ^ flip)) for k in range(2)]
    return lax.ppermute(value, ("z", "c", "yh"), hops)


QUAD = [(0, 0), (4, 0), (0, 1), (4, 1)]
TEXT_BLOCKS = (
    QUAD
    + [(dz + 1, flip) for dz, flip in QUAD]
    + [(dz - 1, flip) for dz, flip in QUAD]
)


def after(values, first):
    return lax.optimization_barrier((values, first))[0]


def matmul(a, b, dims):
    return lax.dot_general(a, b, (dims, ((), ())), preferred_element_type=F32)


STEP = 512
AHEAD = 6
VMEM = pl.BlockSpec(memory_space=pltpu.VMEM)
SMEM = pl.BlockSpec(memory_space=pltpu.SMEM)
HBM = pl.BlockSpec(memory_space=pltpu.HBM)


def weight_copies(up_hbm, down_hbm, up, down, sems):
    steps = up.shape[0]
    ups = [
        pltpu.make_async_copy(up_hbm.at[:, pl.ds(k * STEP, STEP)], up.at[k], sems.at[k]) for k in range(steps)
    ]
    downs = [
        pltpu.make_async_copy(down_hbm.at[pl.ds(k * STEP, STEP)], down.at[k], sems.at[steps + k])
        for k in range(steps)
    ]
    return ups, downs


def split_rows(core, total, mine, others):
    half = mine.shape[0]
    mine[...] = total[pl.ds(pl.multiple_of(core * half, half), half), :]
    others[...] = total[pl.ds(pl.multiple_of((1 - core) * half, half), half), :]


def forward_kernel(core, pooled, text, up_hbm, down_hbm, mine, others, pre_act, text_half, inv_txt, up, down, total, sems):
    ups, downs = weight_copies(up_hbm, down_hbm, up, down, sems)
    order = [copy for both in zip(ups, downs) for copy in both]
    for copy in order[:AHEAD]:
        copy.start()
    full = text[...].astype(F32)
    inv = lax.rsqrt(jnp.sum(full * full, axis=1, keepdims=True) + 1e-06)
    text_half[...] = (full * inv).astype(BF16)
    inv_txt[...] = inv
    activation = pooled[...].astype(F32)
    mean_removed = activation - jnp.mean(activation, axis=1, keepdims=True)
    variance = jnp.mean(mean_removed * mean_removed, axis=1, keepdims=True)
    normed = (mean_removed * lax.rsqrt(variance + 1e-06)).astype(BF16)
    for k in range(len(ups)):
        ups[k].wait()
        for copy in order[2 * k + AHEAD : 2 * k + AHEAD + 1]:
            copy.start()
        pre = matmul(normed, up[k], ((1,), (0,)))
        pre_act[:, pl.ds(k * STEP, STEP)] = pre
        hidden = jax.nn.gelu(pre).astype(BF16)
        downs[k].wait()
        for copy in order[2 * k + AHEAD + 1 : 2 * k + AHEAD + 2]:
            copy.start()
        part = matmul(hidden, down[k], ((1,), (0,)))
        total[...] = part if k == 0 else total[...] + part
    split_rows(core[0], total, mine, others)


def backward_kernel(core, grad_mine, grad_others, pre_act, up, down, mine, others, grad, total):
    half = mine.shape[0]
    grad[pl.ds(pl.multiple_of(core[0] * half, half), half), :] = grad_mine[...]
    grad[pl.ds(pl.multiple_of((1 - core[0]) * half, half), half), :] = grad_others[...]
    for k in range(up.shape[1] // STEP):
        part_of = pl.ds(k * STEP, STEP)
        grad_hidden = matmul(grad[...], down[part_of, :], ((1,), (1,)))
        pre = pre_act[:, part_of]
        root = 0.7978845608028654
        bend = jnp.tanh(root * (pre + 0.044715 * (pre * pre * pre)))
        slope = 0.5 * (1.0 + bend) + (0.5 * root) * pre * (1.0 - bend * bend) * (1.0 + 0.134145 * (pre * pre))
        grad_pre = (grad_hidden * slope).astype(BF16)
        part = matmul(grad_pre, up[:, part_of], ((1,), (1,)))
        total[...] = part if k == 0 else total[...] + part
    split_rows(core[0], total, mine, others)


def mlp_scratch(rows, width, hidden):
    steps = hidden // STEP
    return [
        pltpu.VMEM((steps, width, STEP), BF16),
        pltpu.VMEM((steps, STEP, width), BF16),
        pltpu.VMEM((rows, width), F32),
        pltpu.SemaphoreType.DMA((2 * steps,)),
    ]


def mlp_call(kernel, specs, shapes, scratch, flops, grant):
    return pl.pallas_call(
        kernel,
        in_specs=specs,
        out_specs=[VMEM] * len(shapes),
        out_shape=[jax.ShapeDtypeStruct(shape, dtype) for shape, dtype in shapes],
        scratch_shapes=scratch,
        compiler_params=pltpu.CompilerParams(vmem_limit_bytes=grant * 1024 * 1024),
        cost_estimate=pl.CostEstimate(flops=flops, bytes_accessed=10_000_000, transcendentals=0),
    )


def local(pooled, w_up, w_down, text_embed, scale_bias):
    z, x, yl, c, yh = (lax.axis_index(a) for a in ("z", "x", "yl", "c", "yh"))

    rows, width = pooled.shape
    half = rows // 2
    ff = w_up.shape[1]
    core = c.astype(jnp.int32).reshape(1)
    partial_mine, partial_others, pre_act, text_half, inv_txt = mlp_call(
        forward_kernel,
        [SMEM, VMEM, VMEM, HBM, HBM],
        [
            ((half, width), F32),
            ((half, width), F32),
            ((rows, ff), F32),
            (text_embed.shape, BF16),
            ((text_embed.shape[0], 1), F32),
        ],
        mlp_scratch(rows, width, ff),
        24 * rows * width * ff,
        60,
    )(core, pooled, text_embed, w_up, w_down)
    near = [shift(text_half, "z", 4), swap(text_half, "yh"), across(text_half)]
    branch = (partial_mine + swap(partial_others, "c")).astype(BF16)
    activation = lax.dynamic_slice_in_dim(pooled, c * half, half, 0).astype(F32)
    row_mean = jnp.mean(activation, axis=1, keepdims=True)
    mean_removed = activation - row_mean
    variance = jnp.mean(mean_removed * mean_removed, axis=1, keepdims=True)
    inverse_deviation = lax.rsqrt(variance + 1e-06)
    xhat = mean_removed * inverse_deviation
    four = jnp.concatenate(after([text_half] + near, branch), axis=0)
    texts_in = [shift(four, "z", 1), shift(four, "z", -1), apart(four, 2)]
    branch = branch.astype(F32) + swap(branch, "yl").astype(F32)
    resid = activation + branch
    inv_img = lax.rsqrt(jnp.sum(resid * resid, axis=1, keepdims=True) + 1e-06)
    image_emb = resid * inv_img
    image_half = image_emb.astype(BF16)
    rows_own = lax.all_gather(image_half, "x", axis=0, tiled=True)
    rows_other = swap(rows_own, "c")
    texts_in = after(texts_in, rows_own)
    texts = jnp.concatenate([four] + texts_in, axis=0)

    quad = 4 * half
    row = jnp.arange(quad, dtype=jnp.int32)
    group = ((z * 4 + row // half) * 2 + yh) * (2 * half) + row % half
    few = text_half.shape[0]
    col = jnp.arange(texts.shape[0], dtype=jnp.int32)
    back = jnp.asarray([dz for dz, _ in TEXT_BLOCKS + QUAD], jnp.int32)
    back = back + jnp.where(jnp.arange(16) >= 12, 2 - 4 * c, 0)
    flip = jnp.asarray([f for _, f in TEXT_BLOCKS + QUAD], jnp.int32)
    from_z = (z - jnp.repeat(back, few) + 8) % 8
    from_yh = yh ^ jnp.repeat(flip, few)
    text_ids = ((((from_z * 4 + x) * 2 + yl) * 2 + c) * 2 + from_yh) * few + col % few
    logit_scale = jnp.exp(scale_bias[0])

    def coefficients(images, image_ids):
        logits = logit_scale * matmul(images, texts, ((1,), (1,))) + scale_bias[1]
        pair_sign = jnp.where(image_ids[:, None] == text_ids[None, :], 1.0, -1.0).astype(F32)
        pair_grad = -pair_sign * jax.nn.sigmoid(-pair_sign * logits)
        return (pair_grad * logit_scale).astype(BF16)

    coef_own = coefficients(rows_own, group + c * half)
    coef_other = coefficients(after(rows_other, coef_own), group + (1 - c) * half)

    def chosen(blocks):
        return jnp.concatenate(
            [
                lax.dynamic_slice_in_dim(coef_other if other else coef_own, (x - dx + 4) % 4 * half, half, 0)
                for dx, other in blocks
            ],
            axis=0,
        )

    side = 1 - 2 * c
    swapped_emb = swap(matmul(chosen([(0, 1), (-side, 1), (-side, 0), (2, 1)]), texts, ((1,), (0,))), "c")
    own_emb = matmul(chosen([(0, 0), (side, 0), (side, 1), (2, 0)]), texts, ((1,), (0,)))
    grad_unit = matmul(
        jnp.concatenate([coef_own, coef_other], axis=0),
        jnp.concatenate([rows_own, rows_other], axis=0),
        ((0,), (0,)),
    )

    unit_sent = grad_unit.astype(BF16)
    four = 4 * few
    unit_in = [
        shift(unit_sent[four : 2 * four], "z", -1),
        shift(unit_sent[2 * four : 3 * four], "z", 1),
    ]
    pair = 2 * few
    far = [apart(unit_sent[3 * four : 3 * four + pair], -2), apart(unit_sent[3 * four + pair :], -2, 1)]

    grad_emb = own_emb + after(swapped_emb, unit_sent)
    sent = grad_emb.astype(BF16)
    near = sides(sent[half : 3 * half], -1)
    opposite = shift(sent[3 * half :], "x", -2)
    near, opposite, unit_in = lax.optimization_barrier((near, opposite, unit_in))
    below, above = (value.astype(F32) for value in unit_in)
    unit_sum = grad_unit[:four] + below + above
    unit_flipped = swap(unit_sum[pair:].astype(BF16), "yh")
    total = grad_emb[:half] + opposite.astype(F32)
    total = total + near[:half].astype(F32) + swap(near[half:], "c").astype(F32)
    total = total.astype(BF16)
    far = after(far, total)
    unit_sum = unit_sum[:pair] + far[0].astype(F32) + far[1].astype(F32) + unit_flipped.astype(F32)
    unit_sent = unit_sum[few:].astype(BF16)
    unit_far = shift(unit_sent, "z", 4)
    total = total.astype(F32) + swap(total, "yl").astype(F32)
    grad_resid = (total - image_emb * jnp.sum(image_emb * total, axis=1, keepdims=True)) * inv_img
    resid_half = after(grad_resid.astype(BF16), unit_sent)
    normed_mine, normed_others = mlp_call(
        backward_kernel,
        [SMEM, VMEM, VMEM, VMEM, VMEM, VMEM],
        [((half, width), F32), ((half, width), F32)],
        [pltpu.VMEM((rows, width), BF16), pltpu.VMEM((rows, width), F32)],
        10 * rows * width * ff,
        16,
    )(core, resid_half, swap(resid_half, "c"), pre_act, w_up, w_down)
    normed_sum = (normed_mine + swap(normed_others, "c")).astype(BF16)
    normed_sum = normed_sum.astype(F32) + swap(normed_sum, "yl").astype(F32)
    mean_one = jnp.mean(normed_sum, axis=1, keepdims=True)
    mean_two = jnp.mean(normed_sum * xhat, axis=1, keepdims=True)
    mine_out = grad_resid + inverse_deviation * (normed_sum - mean_one - xhat * mean_two)
    other_out = swap(mine_out, "c")
    first = jnp.where(c == 0, mine_out, other_out)
    second = jnp.where(c == 0, other_out, mine_out)
    gradient_pooled_output = jnp.concatenate([first, second], axis=0)

    grad_own = unit_sum[:few] + after(unit_far, mine_out).astype(F32)
    text_unit = text_embed.astype(F32) * inv_txt
    grad_text = (grad_own - text_unit * jnp.sum(text_unit * grad_own, axis=1, keepdims=True)) * inv_txt
    return (gradient_pooled_output, grad_text)


def solution(mesh):
    fine = Mesh(mesh.devices.reshape(8, 4, 2, 2, 2), ("z", "x", "yl", "c", "yh"))
    images = P(("z", "x", "yh"), None)
    texts = P(("z", "x", "yl", "c", "yh"), None)
    return jax.shard_map(
        local,
        mesh=fine,
        in_specs=(images, P(None, ("yl", "c")), P(("yl", "c"), None), texts, P()),
        out_specs=(images, texts),
        check_vma=False,
    )
```

```python
import jax
import jax.numpy as jnp
from jax import lax
from jax.experimental import pallas as pl
from jax.experimental.pallas import tpu as pltpu
from jax.sharding import Mesh, PartitionSpec as P

F32 = jnp.float32
BF16 = jnp.bfloat16


def swap(value, axis):
    return lax.ppermute(value, axis, [(0, 1), (1, 0)])


def shift(value, axis, by):
    count = lax.axis_size(axis)
    return lax.ppermute(value, axis, [(i, (i + by) % count) for i in range(count)])


def across(value):
    return lax.ppermute(
        value, ("z", "yh"), [(2 * i + j, 2 * ((i + 4) % 8) + 1 - j) for i in range(8) for j in range(2)]
    )


def sides(value, by):
    hops = [((i, j), ((i + (by if j == 0 else -by)) % 4, j)) for i in range(4) for j in range(2)]
    return lax.ppermute(value, ("x", "c"), [(2 * a + b, 2 * p + q) for (a, b), (p, q) in hops])


def apart(value, by, flip=0):
    hops = []
    for i in range(8):
        for j in range(2):
            to = (i + (by if j == 0 else -by)) % 8
            hops += [((2 * i + j) * 2 + k, (2 * to + j) * 2 + (k ^ flip)) for k in range(2)]
    return lax.ppermute(value, ("z", "c", "yh"), hops)


QUAD = [(0, 0), (4, 0), (0, 1), (4, 1)]
TEXT_BLOCKS = (
    QUAD
    + [(dz + 1, flip) for dz, flip in QUAD]
    + [(dz - 1, flip) for dz, flip in QUAD]
)


def after(values, first):
    return lax.optimization_barrier((values, first))[0]


def matmul(a, b, dims):
    return lax.dot_general(a, b, (dims, ((), ())), preferred_element_type=F32)


STEP = 512
AHEAD = 6
VMEM = pl.BlockSpec(memory_space=pltpu.VMEM)
SMEM = pl.BlockSpec(memory_space=pltpu.SMEM)
HBM = pl.BlockSpec(memory_space=pltpu.HBM)


def weight_copies(up_hbm, down_hbm, up, down, sems):
    steps = up.shape[0]
    ups = [
        pltpu.make_async_copy(up_hbm.at[:, pl.ds(k * STEP, STEP)], up.at[k], sems.at[k]) for k in range(steps)
    ]
    downs = [
        pltpu.make_async_copy(down_hbm.at[pl.ds(k * STEP, STEP)], down.at[k], sems.at[steps + k])
        for k in range(steps)
    ]
    return ups, downs


def split_rows(core, total, mine, others):
    half = mine.shape[0]
    mine[...] = total[pl.ds(pl.multiple_of(core * half, half), half), :]
    others[...] = total[pl.ds(pl.multiple_of((1 - core) * half, half), half), :]


def forward_kernel(core, pooled, text, up_hbm, down_hbm, mine, others, pre_act, text_half, inv_txt, up, down, total, sems):
    ups, downs = weight_copies(up_hbm, down_hbm, up, down, sems)
    order = [copy for both in zip(ups, downs) for copy in both]
    for copy in order[:AHEAD]:
        copy.start()
    full = text[...].astype(F32)
    inv = lax.rsqrt(jnp.sum(full * full, axis=1, keepdims=True) + 1e-06)
    text_half[...] = (full * inv).astype(BF16)
    inv_txt[...] = inv
    activation = pooled[...].astype(F32)
    mean_removed = activation - jnp.mean(activation, axis=1, keepdims=True)
    variance = jnp.mean(mean_removed * mean_removed, axis=1, keepdims=True)
    normed = (mean_removed * lax.rsqrt(variance + 1e-06)).astype(BF16)
    for k in range(len(ups)):
        ups[k].wait()
        for copy in order[2 * k + AHEAD : 2 * k + AHEAD + 1]:
            copy.start()
        pre = matmul(normed, up[k], ((1,), (0,)))
        pre_act[:, pl.ds(k * STEP, STEP)] = pre
        hidden = jax.nn.gelu(pre).astype(BF16)
        downs[k].wait()
        for copy in order[2 * k + AHEAD + 1 : 2 * k + AHEAD + 2]:
            copy.start()
        part = matmul(hidden, down[k], ((1,), (0,)))
        total[...] = part if k == 0 else total[...] + part
    split_rows(core[0], total, mine, others)


def backward_kernel(core, grad_mine, grad_others, pre_act, up, down, mine, others, grad, total):
    half = mine.shape[0]
    grad[pl.ds(pl.multiple_of(core[0] * half, half), half), :] = grad_mine[...]
    grad[pl.ds(pl.multiple_of((1 - core[0]) * half, half), half), :] = grad_others[...]
    for k in range(up.shape[1] // STEP):
        part_of = pl.ds(k * STEP, STEP)
        grad_hidden = matmul(grad[...], down[part_of, :], ((1,), (1,)))
        pre = pre_act[:, part_of]
        root = 0.7978845608028654
        bend = jnp.tanh(root * (pre + 0.044715 * (pre * pre * pre)))
        slope = 0.5 * (1.0 + bend) + (0.5 * root) * pre * (1.0 - bend * bend) * (1.0 + 0.134145 * (pre * pre))
        grad_pre = (grad_hidden * slope).astype(BF16)
        part = matmul(grad_pre, up[:, part_of], ((1,), (1,)))
        total[...] = part if k == 0 else total[...] + part
    split_rows(core[0], total, mine, others)


def mlp_scratch(rows, width, hidden):
    steps = hidden // STEP
    return [
        pltpu.VMEM((steps, width, STEP), BF16),
        pltpu.VMEM((steps, STEP, width), BF16),
        pltpu.VMEM((rows, width), F32),
        pltpu.SemaphoreType.DMA((2 * steps,)),
    ]


def mlp_call(kernel, specs, shapes, scratch, flops, grant):
    return pl.pallas_call(
        kernel,
        in_specs=specs,
        out_specs=[VMEM] * len(shapes),
        out_shape=[jax.ShapeDtypeStruct(shape, dtype) for shape, dtype in shapes],
        scratch_shapes=scratch,
        compiler_params=pltpu.CompilerParams(vmem_limit_bytes=grant * 1024 * 1024),
        cost_estimate=pl.CostEstimate(flops=flops, bytes_accessed=10_000_000, transcendentals=0),
    )


def local(pooled, w_up, w_down, text_embed, scale_bias):
    z, x, yl, c, yh = (lax.axis_index(a) for a in ("z", "x", "yl", "c", "yh"))

    rows, width = pooled.shape
    half = rows // 2
    ff = w_up.shape[1]
    core = c.astype(jnp.int32).reshape(1)
    partial_mine, partial_others, pre_act, text_half, inv_txt = mlp_call(
        forward_kernel,
        [SMEM, VMEM, VMEM, HBM, HBM],
        [
            ((half, width), F32),
            ((half, width), F32),
            ((rows, ff), F32),
            (text_embed.shape, BF16),
            ((text_embed.shape[0], 1), F32),
        ],
        mlp_scratch(rows, width, ff),
        24 * rows * width * ff,
        50,
    )(core, pooled, text_embed, w_up, w_down)
    near = [shift(text_half, "z", 4), swap(text_half, "yh"), across(text_half)]
    branch = (partial_mine + swap(partial_others, "c")).astype(BF16)
    activation = lax.dynamic_slice_in_dim(pooled, c * half, half, 0).astype(F32)
    row_mean = jnp.mean(activation, axis=1, keepdims=True)
    mean_removed = activation - row_mean
    variance = jnp.mean(mean_removed * mean_removed, axis=1, keepdims=True)
    inverse_deviation = lax.rsqrt(variance + 1e-06)
    xhat = mean_removed * inverse_deviation
    four = jnp.concatenate(after([text_half] + near, branch), axis=0)
    texts_in = [shift(four, "z", 1), shift(four, "z", -1), apart(four, 2)]
    branch = branch.astype(F32) + swap(branch, "yl").astype(F32)
    resid = activation + branch
    inv_img = lax.rsqrt(jnp.sum(resid * resid, axis=1, keepdims=True) + 1e-06)
    image_emb = resid * inv_img
    image_half = image_emb.astype(BF16)
    rows_own = lax.all_gather(image_half, "x", axis=0, tiled=True)
    rows_other = swap(rows_own, "c")
    texts_in = after(texts_in, rows_own)
    texts = jnp.concatenate([four] + texts_in, axis=0)

    quad = 4 * half
    row = jnp.arange(quad, dtype=jnp.int32)
    group = ((z * 4 + row // half) * 2 + yh) * (2 * half) + row % half
    few = text_half.shape[0]
    col = jnp.arange(texts.shape[0], dtype=jnp.int32)
    back = jnp.asarray([dz for dz, _ in TEXT_BLOCKS + QUAD], jnp.int32)
    back = back + jnp.where(jnp.arange(16) >= 12, 2 - 4 * c, 0)
    flip = jnp.asarray([f for _, f in TEXT_BLOCKS + QUAD], jnp.int32)
    from_z = (z - jnp.repeat(back, few) + 8) % 8
    from_yh = yh ^ jnp.repeat(flip, few)
    text_ids = ((((from_z * 4 + x) * 2 + yl) * 2 + c) * 2 + from_yh) * few + col % few
    logit_scale = jnp.exp(scale_bias[0])

    def coefficients(images, image_ids):
        logits = logit_scale * matmul(images, texts, ((1,), (1,))) + scale_bias[1]
        pair_sign = jnp.where(image_ids[:, None] == text_ids[None, :], 1.0, -1.0).astype(F32)
        pair_grad = -pair_sign * jax.nn.sigmoid(-pair_sign * logits)
        return (pair_grad * logit_scale).astype(BF16)

    coef_own = coefficients(rows_own, group + c * half)
    coef_other = coefficients(after(rows_other, coef_own), group + (1 - c) * half)

    def chosen(blocks):
        return jnp.concatenate(
            [
                lax.dynamic_slice_in_dim(coef_other if other else coef_own, (x - dx + 4) % 4 * half, half, 0)
                for dx, other in blocks
            ],
            axis=0,
        )

    side = 1 - 2 * c
    swapped_emb = swap(matmul(chosen([(0, 1), (-side, 1), (-side, 0), (2, 1)]), texts, ((1,), (0,))), "c")
    own_emb = matmul(chosen([(0, 0), (side, 0), (side, 1), (2, 0)]), texts, ((1,), (0,)))
    grad_unit = matmul(
        jnp.concatenate([coef_own, coef_other], axis=0),
        jnp.concatenate([rows_own, rows_other], axis=0),
        ((0,), (0,)),
    )

    unit_sent = grad_unit.astype(BF16)
    four = 4 * few
    unit_in = [
        shift(unit_sent[four : 2 * four], "z", -1),
        shift(unit_sent[2 * four : 3 * four], "z", 1),
    ]
    pair = 2 * few
    far = [apart(unit_sent[3 * four : 3 * four + pair], -2), apart(unit_sent[3 * four + pair :], -2, 1)]

    grad_emb = own_emb + after(swapped_emb, unit_sent)
    sent = grad_emb.astype(BF16)
    near = sides(sent[half : 3 * half], -1)
    opposite = shift(sent[3 * half :], "x", -2)
    near, opposite, unit_in = lax.optimization_barrier((near, opposite, unit_in))
    below, above = (value.astype(F32) for value in unit_in)
    unit_sum = grad_unit[:four] + below + above
    unit_sent = unit_sum[pair:].astype(BF16)
    total = grad_emb[:half] + opposite.astype(F32)
    total = total + near[:half].astype(F32) + swap(near[half:], "c").astype(F32)
    total = total.astype(BF16)
    far = after(far, total)
    total = total.astype(F32) + swap(total, "yl").astype(F32)
    unit_sum = unit_sum[:pair] + far[0].astype(F32) + far[1].astype(F32)
    unit_flipped = swap(after(unit_sent, total), "yh")
    grad_resid = (total - image_emb * jnp.sum(image_emb * total, axis=1, keepdims=True)) * inv_img
    resid_half = after(grad_resid.astype(BF16), unit_sum)
    normed_mine, normed_others = mlp_call(
        backward_kernel,
        [SMEM, VMEM, VMEM, VMEM, VMEM, VMEM],
        [((half, width), F32), ((half, width), F32)],
        [pltpu.VMEM((rows, width), BF16), pltpu.VMEM((rows, width), F32)],
        10 * rows * width * ff,
        16,
    )(core, resid_half, swap(resid_half, "c"), pre_act, w_up, w_down)
    normed_others, unit_flipped = lax.optimization_barrier((normed_others, unit_flipped))
    unit_sum = unit_sum + unit_flipped.astype(F32)
    unit_far = shift(unit_sum[few:].astype(BF16), "z", 4)
    normed_sum = (normed_mine + swap(normed_others, "c")).astype(BF16)
    normed_sum = normed_sum.astype(F32) + swap(normed_sum, "yl").astype(F32)
    mean_one = jnp.mean(normed_sum, axis=1, keepdims=True)
    mean_two = jnp.mean(normed_sum * xhat, axis=1, keepdims=True)
    mine_out = grad_resid + inverse_deviation * (normed_sum - mean_one - xhat * mean_two)
    other_out = swap(mine_out, "c")
    first = jnp.where(c == 0, mine_out, other_out)
    second = jnp.where(c == 0, other_out, mine_out)
    gradient_pooled_output = jnp.concatenate([first, second], axis=0)

    grad_own = unit_sum[:few] + after(unit_far, mine_out).astype(F32)
    text_unit = text_embed.astype(F32) * inv_txt
    grad_text = (grad_own - text_unit * jnp.sum(text_unit * grad_own, axis=1, keepdims=True)) * inv_txt
    return (gradient_pooled_output, grad_text)


def solution(mesh):
    fine = Mesh(mesh.devices.reshape(8, 4, 2, 2, 2), ("z", "x", "yl", "c", "yh"))
    images = P(("z", "x", "yh"), None)
    texts = P(("z", "x", "yl", "c", "yh"), None)
    return jax.shard_map(
        local,
        mesh=fine,
        in_specs=(images, P(None, ("yl", "c")), P(("yl", "c"), None), texts, P()),
        out_specs=(images, texts),
        check_vma=False,
    )
```

```python
import jax
import jax.numpy as jnp
from jax import lax
from jax.experimental import pallas as pl
from jax.experimental.pallas import tpu as pltpu
from jax.sharding import Mesh, PartitionSpec as P

F32 = jnp.float32
BF16 = jnp.bfloat16


def swap(value, axis):
    return lax.ppermute(value, axis, [(0, 1), (1, 0)])


def shift(value, axis, by):
    count = lax.axis_size(axis)
    return lax.ppermute(value, axis, [(i, (i + by) % count) for i in range(count)])


def across(value):
    return lax.ppermute(
        value, ("z", "yh"), [(2 * i + j, 2 * ((i + 4) % 8) + 1 - j) for i in range(8) for j in range(2)]
    )


def sides(value, by):
    hops = [((i, j), ((i + (by if j == 0 else -by)) % 4, j)) for i in range(4) for j in range(2)]
    return lax.ppermute(value, ("x", "c"), [(2 * a + b, 2 * p + q) for (a, b), (p, q) in hops])


def apart(value, by, flip=0):
    hops = []
    for i in range(8):
        for j in range(2):
            to = (i + (by if j == 0 else -by)) % 8
            hops += [((2 * i + j) * 2 + k, (2 * to + j) * 2 + (k ^ flip)) for k in range(2)]
    return lax.ppermute(value, ("z", "c", "yh"), hops)


QUAD = [(0, 0), (4, 0), (0, 1), (4, 1)]
TEXT_BLOCKS = (
    QUAD
    + [(dz + 1, flip) for dz, flip in QUAD]
    + [(dz - 1, flip) for dz, flip in QUAD]
)


def after(values, first):
    return lax.optimization_barrier((values, first))[0]


def matmul(a, b, dims):
    return lax.dot_general(a, b, (dims, ((), ())), preferred_element_type=F32)


STEP = 768
AHEAD = 6
VMEM = pl.BlockSpec(memory_space=pltpu.VMEM)
SMEM = pl.BlockSpec(memory_space=pltpu.SMEM)
HBM = pl.BlockSpec(memory_space=pltpu.HBM)


def weight_copies(up_hbm, down_hbm, up, down, sems):
    steps = up.shape[0]
    ups = [
        pltpu.make_async_copy(up_hbm.at[:, pl.ds(k * STEP, STEP)], up.at[k], sems.at[k]) for k in range(steps)
    ]
    downs = [
        pltpu.make_async_copy(down_hbm.at[pl.ds(k * STEP, STEP)], down.at[k], sems.at[steps + k])
        for k in range(steps)
    ]
    return ups, downs


def split_rows(core, total, mine, others):
    half = mine.shape[0]
    mine[...] = total[pl.ds(pl.multiple_of(core * half, half), half), :]
    others[...] = total[pl.ds(pl.multiple_of((1 - core) * half, half), half), :]


def forward_kernel(core, pooled, text, up_hbm, down_hbm, mine, others, pre_act, text_half, inv_txt, up, down, total, sems):
    ups, downs = weight_copies(up_hbm, down_hbm, up, down, sems)
    order = [copy for both in zip(ups, downs) for copy in both]
    for copy in order[:AHEAD]:
        copy.start()
    full = text[...].astype(F32)
    inv = lax.rsqrt(jnp.sum(full * full, axis=1, keepdims=True) + 1e-06)
    text_half[...] = (full * inv).astype(BF16)
    inv_txt[...] = inv
    activation = pooled[...].astype(F32)
    mean_removed = activation - jnp.mean(activation, axis=1, keepdims=True)
    variance = jnp.mean(mean_removed * mean_removed, axis=1, keepdims=True)
    normed = (mean_removed * lax.rsqrt(variance + 1e-06)).astype(BF16)
    for k in range(len(ups)):
        ups[k].wait()
        for copy in order[2 * k + AHEAD : 2 * k + AHEAD + 1]:
            copy.start()
        pre = matmul(normed, up[k], ((1,), (0,)))
        pre_act[:, pl.ds(k * STEP, STEP)] = pre
        hidden = jax.nn.gelu(pre).astype(BF16)
        downs[k].wait()
        for copy in order[2 * k + AHEAD + 1 : 2 * k + AHEAD + 2]:
            copy.start()
        part = matmul(hidden, down[k], ((1,), (0,)))
        total[...] = part if k == 0 else total[...] + part
    split_rows(core[0], total, mine, others)


def backward_kernel(core, grad_mine, grad_others, pre_act, up, down, mine, others, grad, total):
    half = mine.shape[0]
    grad[pl.ds(pl.multiple_of(core[0] * half, half), half), :] = grad_mine[...]
    grad[pl.ds(pl.multiple_of((1 - core[0]) * half, half), half), :] = grad_others[...]
    for k in range(up.shape[1] // STEP):
        part_of = pl.ds(k * STEP, STEP)
        grad_hidden = matmul(grad[...], down[part_of, :], ((1,), (1,)))
        pre = pre_act[:, part_of]
        root = 0.7978845608028654
        bend = jnp.tanh(root * (pre + 0.044715 * (pre * pre * pre)))
        slope = 0.5 * (1.0 + bend) + (0.5 * root) * pre * (1.0 - bend * bend) * (1.0 + 0.134145 * (pre * pre))
        grad_pre = (grad_hidden * slope).astype(BF16)
        part = matmul(grad_pre, up[:, part_of], ((1,), (1,)))
        total[...] = part if k == 0 else total[...] + part
    split_rows(core[0], total, mine, others)


def mlp_scratch(rows, width, hidden):
    steps = hidden // STEP
    return [
        pltpu.VMEM((steps, width, STEP), BF16),
        pltpu.VMEM((steps, STEP, width), BF16),
        pltpu.VMEM((rows, width), F32),
        pltpu.SemaphoreType.DMA((2 * steps,)),
    ]


def mlp_call(kernel, specs, shapes, scratch, flops, grant):
    return pl.pallas_call(
        kernel,
        in_specs=specs,
        out_specs=[VMEM] * len(shapes),
        out_shape=[jax.ShapeDtypeStruct(shape, dtype) for shape, dtype in shapes],
        scratch_shapes=scratch,
        compiler_params=pltpu.CompilerParams(vmem_limit_bytes=grant * 1024 * 1024),
        cost_estimate=pl.CostEstimate(flops=flops, bytes_accessed=10_000_000, transcendentals=0),
    )


def local(pooled, w_up, w_down, text_embed, scale_bias):
    z, x, yl, c, yh = (lax.axis_index(a) for a in ("z", "x", "yl", "c", "yh"))

    rows, width = pooled.shape
    half = rows // 2
    ff = w_up.shape[1]
    core = c.astype(jnp.int32).reshape(1)
    partial_mine, partial_others, pre_act, text_half, inv_txt = mlp_call(
        forward_kernel,
        [SMEM, VMEM, VMEM, HBM, HBM],
        [
            ((half, width), F32),
            ((half, width), F32),
            ((rows, ff), F32),
            (text_embed.shape, BF16),
            ((text_embed.shape[0], 1), F32),
        ],
        mlp_scratch(rows, width, ff),
        24 * rows * width * ff,
        50,
    )(core, pooled, text_embed, w_up, w_down)
    near = [shift(text_half, "z", 4), swap(text_half, "yh"), across(text_half)]
    branch = (partial_mine + swap(partial_others, "c")).astype(BF16)
    activation = lax.dynamic_slice_in_dim(pooled, c * half, half, 0).astype(F32)
    row_mean = jnp.mean(activation, axis=1, keepdims=True)
    mean_removed = activation - row_mean
    variance = jnp.mean(mean_removed * mean_removed, axis=1, keepdims=True)
    inverse_deviation = lax.rsqrt(variance + 1e-06)
    xhat = mean_removed * inverse_deviation
    four = jnp.concatenate(after([text_half] + near, branch), axis=0)
    texts_in = [shift(four, "z", 1), shift(four, "z", -1), apart(four, 2)]
    branch = branch.astype(F32) + swap(branch, "yl").astype(F32)
    resid = activation + branch
    inv_img = lax.rsqrt(jnp.sum(resid * resid, axis=1, keepdims=True) + 1e-06)
    image_emb = resid * inv_img
    image_half = image_emb.astype(BF16)
    rows_own = lax.all_gather(image_half, "x", axis=0, tiled=True)
    rows_other = swap(rows_own, "c")
    texts_in = after(texts_in, rows_own)
    texts = jnp.concatenate([four] + texts_in, axis=0)

    quad = 4 * half
    row = jnp.arange(quad, dtype=jnp.int32)
    group = ((z * 4 + row // half) * 2 + yh) * (2 * half) + row % half
    few = text_half.shape[0]
    col = jnp.arange(texts.shape[0], dtype=jnp.int32)
    back = jnp.asarray([dz for dz, _ in TEXT_BLOCKS + QUAD], jnp.int32)
    back = back + jnp.where(jnp.arange(16) >= 12, 2 - 4 * c, 0)
    flip = jnp.asarray([f for _, f in TEXT_BLOCKS + QUAD], jnp.int32)
    from_z = (z - jnp.repeat(back, few) + 8) % 8
    from_yh = yh ^ jnp.repeat(flip, few)
    text_ids = ((((from_z * 4 + x) * 2 + yl) * 2 + c) * 2 + from_yh) * few + col % few
    logit_scale = jnp.exp(scale_bias[0])

    def coefficients(images, image_ids):
        logits = logit_scale * matmul(images, texts, ((1,), (1,))) + scale_bias[1]
        pair_sign = jnp.where(image_ids[:, None] == text_ids[None, :], 1.0, -1.0).astype(F32)
        pair_grad = -pair_sign * jax.nn.sigmoid(-pair_sign * logits)
        return (pair_grad * logit_scale).astype(BF16)

    coef_own = coefficients(rows_own, group + c * half)
    coef_other = coefficients(after(rows_other, coef_own), group + (1 - c) * half)

    def chosen(blocks):
        return jnp.concatenate(
            [
                lax.dynamic_slice_in_dim(coef_other if other else coef_own, (x - dx + 4) % 4 * half, half, 0)
                for dx, other in blocks
            ],
            axis=0,
        )

    side = 1 - 2 * c
    swapped_emb = swap(matmul(chosen([(0, 1), (-side, 1), (-side, 0), (2, 1)]), texts, ((1,), (0,))), "c")
    own_emb = matmul(chosen([(0, 0), (side, 0), (side, 1), (2, 0)]), texts, ((1,), (0,)))
    grad_unit = matmul(
        jnp.concatenate([coef_own, coef_other], axis=0),
        jnp.concatenate([rows_own, rows_other], axis=0),
        ((0,), (0,)),
    )

    unit_sent = grad_unit.astype(BF16)
    four = 4 * few
    unit_in = [
        shift(unit_sent[four : 2 * four], "z", -1),
        shift(unit_sent[2 * four : 3 * four], "z", 1),
    ]
    pair = 2 * few
    far = [apart(unit_sent[3 * four : 3 * four + pair], -2), apart(unit_sent[3 * four + pair :], -2, 1)]

    grad_emb = own_emb + after(swapped_emb, unit_sent)
    sent = grad_emb.astype(BF16)
    near = sides(sent[half : 3 * half], -1)
    opposite = shift(sent[3 * half :], "x", -2)
    near, opposite, unit_in = lax.optimization_barrier((near, opposite, unit_in))
    below, above = (value.astype(F32) for value in unit_in)
    unit_sum = grad_unit[:four] + below + above
    unit_sent = unit_sum[pair:].astype(BF16)
    total = grad_emb[:half] + opposite.astype(F32)
    total = total + near[:half].astype(F32) + swap(near[half:], "c").astype(F32)
    total = total.astype(BF16)
    far = after(far, total)
    total = total.astype(F32) + swap(total, "yl").astype(F32)
    unit_sum = unit_sum[:pair] + far[0].astype(F32) + far[1].astype(F32)
    unit_flipped = swap(after(unit_sent, total), "yh")
    grad_resid = (total - image_emb * jnp.sum(image_emb * total, axis=1, keepdims=True)) * inv_img
    resid_half = after(grad_resid.astype(BF16), unit_sum)
    normed_mine, normed_others = mlp_call(
        backward_kernel,
        [SMEM, VMEM, VMEM, VMEM, VMEM, VMEM],
        [((half, width), F32), ((half, width), F32)],
        [pltpu.VMEM((rows, width), BF16), pltpu.VMEM((rows, width), F32)],
        10 * rows * width * ff,
        16,
    )(core, resid_half, swap(resid_half, "c"), pre_act, w_up, w_down)
    normed_others, unit_flipped = lax.optimization_barrier((normed_others, unit_flipped))
    unit_sum = unit_sum + unit_flipped.astype(F32)
    unit_far = shift(unit_sum[few:].astype(BF16), "z", 4)
    normed_sum = (normed_mine + swap(normed_others, "c")).astype(BF16)
    normed_sum = normed_sum.astype(F32) + swap(normed_sum, "yl").astype(F32)
    mean_one = jnp.mean(normed_sum, axis=1, keepdims=True)
    mean_two = jnp.mean(normed_sum * xhat, axis=1, keepdims=True)
    mine_out = grad_resid + inverse_deviation * (normed_sum - mean_one - xhat * mean_two)
    other_out = swap(mine_out, "c")
    first = jnp.where(c == 0, mine_out, other_out)
    second = jnp.where(c == 0, other_out, mine_out)
    gradient_pooled_output = jnp.concatenate([first, second], axis=0)

    grad_own = unit_sum[:few] + after(unit_far, mine_out).astype(F32)
    text_unit = text_embed.astype(F32) * inv_txt
    grad_text = (grad_own - text_unit * jnp.sum(text_unit * grad_own, axis=1, keepdims=True)) * inv_txt
    return (gradient_pooled_output, grad_text)


def solution(mesh):
    fine = Mesh(mesh.devices.reshape(8, 4, 2, 2, 2), ("z", "x", "yl", "c", "yh"))
    images = P(("z", "x", "yh"), None)
    texts = P(("z", "x", "yl", "c", "yh"), None)
    return jax.shard_map(
        local,
        mesh=fine,
        in_specs=(images, P(None, ("yl", "c")), P(("yl", "c"), None), texts, P()),
        out_specs=(images, texts),
        check_vma=False,
    )
```
